32 devices in a mesh: row: 8 (over y, x, core), col: 4 (over z).
Axes of the slice: x: 2, y: 2, z: 4, core: 2. Of those that a mesh axis runs over, the one named last changes fastest.
Arguments:
- amps: float32 [32, 4, 576, 576], P(None, None, 'row', 'col'), may hold values from -6 to 6
- integrals: float32 [4, 576, 32, 576], P(None, 'row', 'col'), may hold values from -0.5 to 0.5
- e_occ: float32 [32], replicated, may hold values from -2 to -0.5
- e_vir: float32 [576], replicated, may hold values from 0.5 to 3
Outputs:
- update: float32 [32, 32, 576, 576], P('row', 'col')
The draws below stay inside these ranges and needn't reach their ends.
All inputs are finite; a program needn't handle non-finite values.
Results may differ from the reference program's by a relative error of at most 0.00007.
Values sent between devices are 32-bit elements; how exact they have to be, the bound alone decides.
A program may use at most 256 MiB of HBM per device.

```python
import jax
import jax.numpy as jnp
from jax import lax

O = 32
V = 576
KW = 4


def steps_of(rng, dims, shards, least, top_value):
    factor_of, own = 1.0, jax.random.fold_in(rng, 6)
    for position, blocks in shards:
        heights = jnp.exp(jax.random.uniform(jax.random.fold_in(own, position), (blocks,), jnp.float32, least / len(shards), top_value / len(shards)))
        factor_of = factor_of * jnp.repeat(heights, dims[position] // blocks).reshape([-1 if axis == position else 1 for axis in range(len(dims))])
    return factor_of


def bell_draw(rng, extent, deviation, bound, pieces=(), kind=jnp.bfloat16):
    level = steps_of(rng, extent, pieces, -0.22, 0.18) if pieces else 1.0
    values = jax.random.normal(rng, extent, jnp.float32) * deviation * level
    return jnp.minimum(jnp.maximum(values, -bound), bound).astype(kind)


def setup_inputs(seed: int = 0) -> dict:
    streams_of = jax.random.split(jax.random.key(seed), 5)
    amps = bell_draw(streams_of[0], (O, KW, V, V), 1.0, 6.0, ((2, 8), (3, 4)), jnp.float32)
    integrals = bell_draw(streams_of[1], (KW, V, O, V), (KW * V // 16) ** -0.5, 0.5, ((1, 8), (2, 4)), jnp.float32)
    e_occ = jnp.clip(jax.random.uniform(streams_of[2], (O,), jnp.float32, -2.0, -0.5), -2.0, -0.5)
    e_vir = jnp.clip(jax.random.uniform(streams_of[3], (V,), jnp.float32, 0.5, 3.0), 0.5, 3.0)
    return dict(amps=amps, integrals=integrals, e_occ=e_occ, e_vir=e_vir)


def reference(amps, integrals, e_occ, e_vir):
    def one_index(pair):
        amp_block, energy = pair
        contracted = jnp.einsum("kac,kcjb->jab", amp_block.astype(jnp.float32), integrals.astype(jnp.float32), precision=lax.Precision.HIGHEST)
        denom = energy + e_occ[:, None, None] - e_vir[None, :, None] - e_vir[None, None, :]
        return contracted / denom

    return lax.map(one_index, (amps, e_occ))
```

```python
import jax
import jax.numpy as jnp
from jax import lax
from jax.sharding import PartitionSpec as P


def contract(left, right):
    return jnp.einsum(
        "ikac,kcjb->ijab",
        left,
        right,
        precision=lax.Precision.HIGH,
        preferred_element_type=jnp.float32,
    )


def shards(amps, integrals, e_occ, e_vir):
    row_count = lax.axis_size("row")
    col_count = lax.axis_size("col")
    row_index = lax.axis_index("row")
    col_index = lax.axis_index("col")
    occ_col = e_occ.shape[0] // col_count
    occ_row = e_occ.shape[0] // row_count
    i_energy = lax.dynamic_slice_in_dim(e_occ, row_index * occ_row, occ_row)
    j_energy = lax.dynamic_slice_in_dim(e_occ, col_index * occ_col, occ_col)
    by_owner = amps.reshape((row_count, occ_row) + amps.shape[1:])

    def exchange(source, i):
        return lax.all_to_all(source[:, i], "row", split_axis=0, concat_axis=2, tiled=True)

    def widen(left):
        return lax.all_gather(left, "col", axis=3, tiled=True)

    first = exchange(by_owner, 0)
    first, by_owner = lax.optimization_barrier((first, by_owner))
    lefts = [first] + [exchange(by_owner, i) for i in range(1, occ_row)]
    whole = widen(first)
    whole, integrals = lax.optimization_barrier((whole, integrals))
    gathered = lax.all_gather(integrals, "row", axis=1, tiled=True)
    pair = e_vir[:, None] + e_vir[None, :]
    virtuals = e_vir.shape[0]
    out = jnp.zeros((occ_row, occ_col, virtuals, virtuals), jnp.float32)
    update = None
    for i in range(occ_row):
        later = None
        if i + 1 < occ_row:
            if update is None:
                left, gathered = lax.optimization_barrier((lefts[i + 1], gathered))
            else:
                left, update = lax.optimization_barrier((lefts[i + 1], update))
            later = widen(left)
        if update is not None:
            out = lax.dynamic_update_slice(out, update, (i - 1, 0, 0, 0))
        denom = (i_energy[i] + j_energy)[None, :, None, None] - pair[None, None]
        update = contract(whole, gathered) / denom
        whole = later
    return lax.dynamic_update_slice(out, update, (occ_row - 1, 0, 0, 0))


def solution(mesh):
    placed = (P(None, None, "row", "col"), P(None, "row", "col", None), P(), P())
    return jax.shard_map(
        shards, mesh=mesh, in_specs=placed, out_specs=P("row", "col", None, None), check_vma=False
    )
```
